32 devices in a mesh: chan: 8 (over z, x), tm: 4 (over y, core).
Axes of the slice: x: 2, y: 2, z: 4, core: 2. Of those that a mesh axis runs over, the one named last changes fastest.
Arguments:
- traces: bfloat16 [32, 2048, 256], P('tm', 'chan')
- tile_list: int32 [8, 2], P('chan'), may hold values from 0 to 7, as said below
- seg_counts: int32 [8], P('chan'), may hold values from 0 to 32, as said below
Outputs:
- correlations: bfloat16 [8, 256, 256, 128], P('chan', 'tm')
The draws below stay inside these ranges and needn't reach their ends.
Inputs may be any that keep to these rules, and one draw needn't show every extreme that they name: `tile_list`: for a slot of chan index c, the row block lies within c - 1 .. c + 1 and the column block lies within row block .. row block + 1 and within c - 1 .. c + 1; both are valid block numbers, and 0 and 7 are both used. `seg_counts`: A count of 0 marks an empty slot; both ends are reached.
All inputs are finite; a program needn't handle non-finite values.
Results may differ from the reference program's by a relative error of at most 0.0076.
Values may be sent and summed in bfloat16 or wider, within the bound.
A program may use at most 128 MiB of HBM per device.

```python
import math
import jax
import jax.numpy as jnp
from jax import lax

BLOCK = 256
SAMP = 256
NF = 128
LAGS = 128
MAXT = 1
NSEG = 32
CHANNELS = 2048
SLOTS = 8


def draw_traces(key, part):
    key = jax.random.fold_in(key, 1)
    key_base, key_chan = jax.random.split(key, 2)
    chan_scale = jnp.exp(jax.random.uniform(key_chan, (1, CHANNELS, 1), jnp.float32, 0.0, math.log(10.0)))
    ramp = 1.0 + 2.0 * jnp.arange(NSEG, dtype=jnp.float32) / max(NSEG - 1, 1)
    ramp = ramp[:, None, None]
    base = jax.random.normal(key_base, (NSEG, CHANNELS, SAMP), jnp.float32)
    return (base * chan_scale * ramp).astype(jnp.bfloat16)


def draw_tile_list(key, part):
    key = jax.random.fold_in(key, 2)
    key_off, key_step = jax.random.split(key, 2)
    nblocks = CHANNELS // BLOCK
    owner = jnp.arange(SLOTS, dtype=jnp.int32) // MAXT
    lowest = jnp.maximum(owner - 1, 0)
    highest = jnp.minimum(owner + 1, nblocks - 1)
    offset = jax.random.randint(key_off, (SLOTS,), -1, 2, jnp.int32)
    offset = offset.at[0].set(0).at[SLOTS - 1].set(0)
    row_b = jnp.clip(owner + offset, lowest, highest)
    step = jax.random.randint(key_step, (SLOTS,), 0, 2, jnp.int32)
    col_b = jnp.minimum(row_b + step, highest)
    return jnp.stack([row_b, col_b], axis=1).astype(jnp.int32)


def draw_seg_counts(key, part):
    key = jax.random.fold_in(key, 3)
    counts = jax.random.randint(key, (SLOTS,), 0, NSEG + 1, jnp.int32)
    counts = counts.at[0].set(NSEG).at[SLOTS - 1].set(0)
    return counts.astype(jnp.int32)


def setup_inputs(seed: int = 0) -> dict:
    key_list = jax.random.split(jax.random.key(seed), 4)
    return {
        "traces": draw_traces(jax.random.fold_in(key_list[3], 71), 0),
        "tile_list": draw_tile_list(jax.random.fold_in(key_list[3], 71), 0),
        "seg_counts": draw_seg_counts(jax.random.fold_in(key_list[3], 71), 0),
    }


def forward_table():
    n_idx = jnp.arange(SAMP, dtype=jnp.int32)[:, None]
    k_idx = jnp.arange(1, NF + 1, dtype=jnp.int32)[None, :]
    phase = (n_idx * k_idx % SAMP).astype(jnp.float32) * (2.0 * math.pi / SAMP)
    return jnp.concatenate([jnp.cos(phase), -jnp.sin(phase)], axis=1).astype(jnp.bfloat16)

def inverse_table():
    k_idx = jnp.arange(1, NF + 1, dtype=jnp.int32)[:, None]
    lag_idx = jnp.arange(LAGS, dtype=jnp.int32)[None, :] - LAGS // 2
    phase = (k_idx * lag_idx % SAMP).astype(jnp.float32) * (2.0 * math.pi / SAMP)
    norm = 1.0 / math.sqrt(NF)
    return (jnp.concatenate([jnp.cos(phase), -jnp.sin(phase)], axis=0) * norm).astype(jnp.bfloat16)

def reference(traces, tile_list, seg_counts):
    nseg = traces.shape[0]
    spectra = jnp.dot(traces.reshape(-1, SAMP), forward_table(), preferred_element_type=jnp.float32)
    spectra = spectra.reshape(nseg, CHANNELS, 2 * NF)
    energy = lax.optimization_barrier(jnp.sum(spectra * spectra, axis=(0, 2)))
    scale = 1.0 / jnp.sqrt(energy / (nseg * NF) + 1e-06)
    white = (spectra * scale[None, :, None]).astype(jnp.bfloat16)
    itable = inverse_table()
    seg_ids = jnp.arange(nseg, dtype=jnp.int32)

    def one_slot(slot):
        row_b = tile_list[slot, 0].astype(jnp.int32)
        col_b = tile_list[slot, 1].astype(jnp.int32)
        count = seg_counts[slot].astype(jnp.int32)
        left = lax.dynamic_slice_in_dim(white, (row_b * BLOCK).astype(jnp.int32), BLOCK, 1)
        right = lax.dynamic_slice_in_dim(white, (col_b * BLOCK).astype(jnp.int32), BLOCK, 1)
        live = (seg_ids < count).astype(jnp.bfloat16)
        left = left * live[:, None, None]
        lre = left[..., :NF].astype(jnp.float32)
        lim = left[..., NF:].astype(jnp.float32)
        rre = right[..., :NF].astype(jnp.float32)
        rim = right[..., NF:].astype(jnp.float32)
        real = jnp.einsum('sif,sjf->ijf', lre, rre) + jnp.einsum('sif,sjf->ijf', lim, rim)
        imag = jnp.einsum('sif,sjf->ijf', lre, rim) - jnp.einsum('sif,sjf->ijf', lim, rre)
        denom = jnp.maximum(count, 1).astype(jnp.float32)
        cross = (jnp.concatenate([real, imag], axis=-1) / denom).astype(jnp.bfloat16)
        corr = jnp.dot(cross.reshape(-1, 2 * NF), itable, preferred_element_type=jnp.float32)
        return corr.reshape(BLOCK, BLOCK, LAGS).astype(jnp.bfloat16)
    return lax.map(one_slot, jnp.arange(SLOTS, dtype=jnp.int32))
```

```python
import functools
import math

import jax
import jax.numpy as jnp
from jax import lax
from jax.experimental import pallas as pl
from jax.experimental.pallas import tpu as pltpu
from jax.sharding import PartitionSpec as P

NF = 128
LAGS = 128
LANES = 128
MESH = pl.DeviceIdType.MESH
F32 = jnp.float32
BF16 = jnp.bfloat16


def forward_table(samples, nbins):
    n_idx = jnp.arange(samples, dtype=jnp.int32)[None, :]
    k_idx = jnp.arange(1, nbins + 1, dtype=jnp.int32)[:, None]
    phase = (n_idx * k_idx % samples).astype(F32) * (2.0 * math.pi / samples)
    return jnp.concatenate([jnp.cos(phase), -jnp.sin(phase)], axis=0).astype(BF16)


def inverse_table(samples, nbins, nlags):
    k_idx = jnp.arange(1, nbins + 1, dtype=jnp.int32)[None, :]
    lag_idx = jnp.arange(nlags, dtype=jnp.int32)[:, None] - nlags // 2
    phase = (k_idx * lag_idx % samples).astype(F32) * (2.0 * math.pi / samples)
    norm = 1.0 / math.sqrt(nbins)
    return (jnp.concatenate([jnp.cos(phase), -jnp.sin(phase)], axis=1) * norm).astype(BF16)


def pick(flag, yes, no):
    return jnp.where(flag > 0, yes.astype(F32), no.astype(F32)).astype(BF16)


def exchange(nchan, x_ref, flag_ref, r_ref, l_ref, far, near, got, lsend, wish,
             a_send, a_recv, b_send, b_recv, w_send, w_recv,
             r_send, r_recv, l_send, l_recv):
    segs, block, samples = x_ref.shape
    rows = block // 4
    c = lax.axis_index("chan")
    t = lax.axis_index("tm")
    odd = lax.rem(c, 2)
    partner = c + 1 - 2 * odd
    z_to = lax.rem(c + nchan - 2 + 4 * odd, nchan)
    z_from = lax.rem(c + nchan + 2 - 4 * odd, nchan)
    core = lax.rem(t, 2)
    t1 = t + 1 - 2 * core
    t2 = lax.rem(t + 2, 4)
    t3 = lax.rem(t1 + 2, 4)

    barrier = pltpu.get_barrier_semaphore()
    for where in ((z_to, t), (z_from, t), (partner, t), (c, t1), (c, t2), (c, t3)):
        pl.semaphore_signal(barrier, inc=1, device_id=where, device_id_type=MESH)
    pl.semaphore_wait(barrier, 6)

    def send(src, dst, ss, rs, where):
        return pltpu.make_async_remote_copy(
            src_ref=src, dst_ref=dst, send_sem=ss, recv_sem=rs,
            device_id=where, device_id_type=MESH)

    ask = send(flag_ref.at[pl.ds(0, 8)], wish, w_send, w_recv, (partner, t))
    ask.start()
    hop_a = [send(x_ref.at[k], far.at[k], a_send.at[k], a_recv.at[k], (z_to, t))
             for k in range(segs)]
    hop_b = [send(near.at[k], got.at[k], b_send.at[k], b_recv.at[k], (partner, t))
             for k in range(segs)]

    def share(k, slot, which, where):
        ref = r_ref.at[slot * segs + k]
        return send(ref, ref, r_send.at[which, k], r_recv.at[which, k], where)

    def share_l(k, which, peer):
        return send(lsend.at[k, pl.ds(pl.multiple_of(peer * rows, rows), rows)],
                    l_ref.at[t * segs + k],
                    l_send.at[which, k], l_recv.at[which, k], (c, peer))

    to_y = [share(k, t, 0, (c, t2)) for k in range(segs)]
    to_core = [share(k, t, 1, (c, t1)) for k in range(segs)]
    forward = [share(k, t2, 2, (c, t1)) for k in range(segs)]
    parts = [[share_l(k, w, p) for w, p in enumerate((t2, t3, t1))] for k in range(segs)]

    for k in range(segs):
        hop_a[k].start()
    ask.wait_recv()
    for step in range(segs + 2):
        k = step
        if k < segs:
            hop_a[k].wait_recv()
            near[k] = pick(wish[0:1, :], far[k], x_ref[k])
            hop_b[k].start()
        k = step - 1
        if 0 <= k < segs:
            hop_b[k].wait_recv()
            r_ref[t * segs + k] = pick(flag_ref[8:9, :], got[k], x_ref[k])
            to_y[k].start()
            lsend[k] = pick(flag_ref[16:17, :], got[k], x_ref[k])
            for copy in parts[k]:
                copy.start()
            to_core[k].start()
            l_ref[t * segs + k] = lsend[k, pl.ds(pl.multiple_of(t * rows, rows), rows)]
        k = step - 2
        if 0 <= k < segs:
            to_y[k].wait_recv()
            forward[k].start()
    ask.wait_send()
    for k in range(segs):
        hop_a[k].wait_send()
        hop_b[k].wait_send()
        to_y[k].wait_send()
        to_core[k].wait()
        forward[k].wait()
        for copy in parts[k]:
            copy.wait()


def correlate(count_ref, r_ref, l_ref, fwd_ref, inv_ref, o_ref, rspec, lspec, cross):
    nseg, block, samples = r_ref.shape
    rows = l_ref.shape[1]
    bins = 2 * NF
    nt = (((1,), (1,)), ((), ()))
    count = count_ref[0]
    lane = lax.broadcasted_iota(jnp.int32, (1, 2 * rows), 1)
    halves = block // LANES
    span = nseg * bins
    depth = NF * 2 * rows

    def spectra(s, carry):
        re, le = carry
        fwd = fwd_ref[...]
        spec = lax.dot_general(fwd, r_ref[s], nt, preferred_element_type=F32)
        base = pl.multiple_of(s * bins, bins)
        for h in range(halves):
            rspec[pl.ds(h * span + base, bins), :] = spec[:, h * LANES:(h + 1) * LANES]
        re = re + jnp.sum((spec * spec).reshape(bins // 8, 8, block), axis=0)
        left = l_ref[s]
        both = jnp.concatenate([left, left], axis=0)
        spec = lax.dot_general(fwd, both, nt, preferred_element_type=F32)
        le = le + jnp.sum((spec * spec).reshape(bins // 8, 8, 2 * rows), axis=0)
        top, bottom = spec[:NF], spec[NF:]
        lspec[pl.ds(base, NF), :] = jnp.where(lane < rows, top, -bottom)
        lspec[pl.ds(base + NF, NF), :] = jnp.where(lane < rows, bottom, top)
        return re, le

    re, le = lax.fori_loop(
        0, nseg, spectra,
        (jnp.zeros((8, block), F32), jnp.zeros((8, 2 * rows), F32)))
    rscale = 1.0 / jnp.sqrt(jnp.sum(re, axis=0, keepdims=True) / (nseg * NF) + 1e-06)
    lscale = 1.0 / jnp.sqrt(jnp.sum(le, axis=0, keepdims=True) / (nseg * NF) + 1e-06)
    seg_of = lax.broadcasted_iota(jnp.int32, (2 * nseg, 2 * rows), 0) // 2
    lscale = jnp.where(seg_of < count, jnp.broadcast_to(lscale, (2 * nseg, 2 * rows)), 0.0)

    def one_bin(f, _):
        right = jnp.concatenate(
            [rspec[pl.ds(h * span + f, 2 * nseg, stride=NF), :] for h in range(halves)], axis=1)
        right = (right * rscale).astype(BF16)
        left = (lspec[pl.ds(f, 2 * nseg, stride=NF), :] * lscale).astype(BF16)
        both = lax.dot_general(
            left, right, (((0,), (0,)), ((), ())), preferred_element_type=F32)
        base = pl.multiple_of(f * 2 * rows, 2 * rows)
        for h in range(halves):
            cross[pl.ds(h * depth + base, 2 * rows), :] = both[:, h * LANES:(h + 1) * LANES]
        return 0

    lax.fori_loop(0, NF, one_bin, 0, unroll=4)
    share = 1.0 / jnp.maximum(count, 1).astype(F32)

    def one_row(i, _):
        for h in range(halves):
            real = cross[pl.ds(h * depth + i, NF, stride=2 * rows), :].astype(BF16)
            imag = cross[pl.ds(h * depth + rows + i, NF, stride=2 * rows), :].astype(BF16)
            both = jnp.concatenate([real, imag], axis=0)
            corr = jnp.dot(inv_ref[...], both, preferred_element_type=F32) * share
            o_ref[i, pl.ds(h * LANES, LANES), :] = corr.T.astype(BF16)
        return 0

    lax.fori_loop(0, rows, one_row, 0, unroll=2)


def body(nchan, traces, tile_list, seg_counts):
    segs, block, samples = traces.shape
    ntm = 4
    nseg = segs * ntm
    rows = block // ntm
    c = lax.axis_index("chan")
    row_b, col_b = tile_list[0, 0], tile_list[0, 1]
    beyond = jnp.where(c % 2 == 1, jnp.maximum(row_b, col_b) == c + 1,
                       jnp.minimum(row_b, col_b) == c - 1)
    flags = jnp.stack([beyond, col_b != c, row_b != c]).astype(jnp.int32)
    flags = jnp.broadcast_to(flags[:, None, None], (3, 8, samples)).reshape(24, samples)
    vmem = pl.BlockSpec(memory_space=pltpu.VMEM)
    dma = pltpu.SemaphoreType.DMA
    right, left = pl.pallas_call(
        functools.partial(exchange, nchan),
        out_shape=(jax.ShapeDtypeStruct((nseg, block, samples), BF16),
                   jax.ShapeDtypeStruct((nseg, rows, samples), BF16)),
        in_specs=[vmem, vmem],
        out_specs=(vmem, vmem),
        scratch_shapes=[pltpu.VMEM((segs, block, samples), BF16)] * 4 + [
            pltpu.VMEM((8, samples), jnp.int32),
            dma((segs,)), dma((segs,)), dma((segs,)), dma((segs,)), dma, dma,
            dma((3, segs)), dma((3, segs)), dma((3, segs)), dma((3, segs))],
        compiler_params=pltpu.CompilerParams(
            collective_id=0, has_side_effects=True, vmem_limit_bytes=32 << 20),
        name="exchange",
    )(traces, flags)
    out = pl.pallas_call(
        correlate,
        out_shape=jax.ShapeDtypeStruct((rows, block, LAGS), BF16),
        in_specs=[pl.BlockSpec(memory_space=pltpu.SMEM), vmem, vmem, vmem, vmem],
        out_specs=vmem,
        scratch_shapes=[pltpu.VMEM((block // LANES * nseg * 2 * NF, LANES), F32),
                        pltpu.VMEM((nseg * 2 * NF, 2 * rows), F32),
                        pltpu.VMEM((block // LANES * NF * 2 * rows, LANES), F32)],
        compiler_params=pltpu.CompilerParams(vmem_limit_bytes=56 << 20),
        name="correlate",
    )(seg_counts, right, left, forward_table(samples, NF), inverse_table(samples, NF, LAGS))
    return out[None]


def solution(mesh):
    return jax.shard_map(
        functools.partial(body, mesh.shape["chan"]),
        mesh=mesh,
        in_specs=(P("tm", "chan", None), P("chan", None), P("chan")),
        out_specs=P("chan", "tm", None, None),
        check_vma=False,
    )
```

```python
import functools
import math

import jax
import jax.numpy as jnp
import numpy as np
from jax import lax
from jax.experimental import pallas as pl
from jax.experimental.pallas import tpu as pltpu
from jax.sharding import PartitionSpec as P

NF = 128
LAGS = 128
LANES = 128
PITCH = NF + 8
MESH = pl.DeviceIdType.MESH
F32 = jnp.float32
BF16 = jnp.bfloat16


def forward_table(samples, nbins):
    n_idx = np.arange(samples)[None, :]
    k_idx = np.arange(1, nbins + 1)[:, None]
    phase = (n_idx * k_idx % samples).astype(np.float32) * np.float32(2.0 * math.pi / samples)
    return jnp.asarray(np.concatenate([np.cos(phase), -np.sin(phase)], axis=0), BF16)


def inverse_table(samples, nbins, nlags):
    k_idx = np.arange(1, nbins + 1)[None, :]
    lag_idx = np.arange(nlags)[:, None] - nlags // 2
    phase = (k_idx * lag_idx % samples).astype(np.float32) * np.float32(2.0 * math.pi / samples)
    norm = np.float32(1.0 / math.sqrt(nbins))
    return jnp.asarray(np.concatenate([np.cos(phase), -np.sin(phase)], axis=1) * norm, BF16)


def pick(flag, yes, no):
    return jnp.where(flag > 0, yes.astype(F32), no.astype(F32)).astype(BF16)


def kernel(nchan, tile_ref, count_ref, x_ref, fwd_ref, inv_ref, o_ref,
           own, far, near, got, lsend, asked, wish, r_ref, l_ref, rspec, lspec, renergy, lenergy,
           cross, out, own_sem, a_send, a_recv, b_send, b_recv, w_send, w_recv,
           r_send, r_recv, l_send, l_recv, o_sem):
    segs, block, samples = own.shape
    nseg = r_ref.shape[0]
    rows = block // 4
    halves = block // LANES
    span = nseg * 2 * PITCH
    depth = NF * PITCH
    c = lax.axis_index("chan")
    t = lax.axis_index("tm")
    odd = lax.rem(c, 2)
    partner = c + 1 - 2 * odd
    z_to = lax.rem(c + nchan - 2 + 4 * odd, nchan)
    z_from = lax.rem(c + nchan + 2 - 4 * odd, nchan)
    core = lax.rem(t, 2)
    t1 = t + 1 - 2 * core
    t2 = lax.rem(t + 2, 4)
    t3 = lax.rem(t1 + 2, 4)

    mine = [pltpu.make_async_copy(x_ref.at[k], own.at[k], own_sem.at[k]) for k in range(segs)]
    for copy in mine:
        copy.start()
    row_b, col_b = tile_ref[0, 0], tile_ref[0, 1]
    beyond = jnp.where(odd == 1, jnp.maximum(row_b, col_b) - c, c - jnp.minimum(row_b, col_b))
    asked[...] = jnp.full(asked.shape, beyond, jnp.int32)
    take_r = jnp.full((1, samples), (col_b - c) * (col_b - c), jnp.int32)
    take_l = jnp.full((1, samples), (row_b - c) * (row_b - c), jnp.int32)
    renergy[...] = jnp.zeros_like(renergy)
    lenergy[...] = jnp.zeros_like(lenergy)

    barrier = pltpu.get_barrier_semaphore()
    for where in ((z_to, t), (z_from, t), (partner, t), (c, t1), (c, t2), (c, t3)):
        pl.semaphore_signal(barrier, inc=1, device_id=where, device_id_type=MESH)
    pl.semaphore_wait(barrier, 6)

    def send(src, dst, ss, rs, where):
        return pltpu.make_async_remote_copy(
            src_ref=src, dst_ref=dst, send_sem=ss, recv_sem=rs,
            device_id=where, device_id_type=MESH)

    ask = send(asked, wish, w_send, w_recv, (partner, t))
    ask.start()
    hop_a = [send(x_ref.at[k], far.at[k], a_send.at[k], a_recv.at[k], (z_to, t))
             for k in range(segs)]
    hop_b = [send(near.at[k], got.at[k], b_send.at[k], b_recv.at[k], (partner, t))
             for k in range(segs)]

    def share(k, slot, which, where):
        ref = r_ref.at[slot * segs + k]
        return send(ref, ref, r_send.at[which, k], r_recv.at[which, k], where)

    def share_l(k, which, peer):
        return send(lsend.at[k, pl.ds(pl.multiple_of(peer * rows, rows), rows)],
                    l_ref.at[t * segs + k],
                    l_send.at[which, k], l_recv.at[which, k], (c, peer))

    to_y = [share(k, t, 0, (c, t2)) for k in range(segs)]
    to_core = [share(k, t, 1, (c, t1)) for k in range(segs)]
    forward = [share(k, t2, 2, (c, t1)) for k in range(segs)]
    parts = [[share_l(k, w, p) for w, p in enumerate((t2, t3, t1))] for k in range(segs)]

    nt = (((1,), (1,)), ((), ()))
    lane = lax.broadcasted_iota(jnp.int32, (1, 2 * rows), 1)

    def spectra_r(s):
        spec = lax.dot_general(fwd_ref[...], r_ref[s], nt, preferred_element_type=F32)
        base = pl.multiple_of(s * 2 * PITCH, 8)
        for h in range(halves):
            cols = slice(h * LANES, (h + 1) * LANES)
            rspec[pl.ds(h * span + base, NF), :] = spec[:NF, cols]
            rspec[pl.ds(h * span + base + PITCH, NF), :] = spec[NF:, cols]
        renergy[...] += jnp.sum((spec * spec).reshape(2 * NF // 8, 8, block), axis=0)

    def spectra_l(s):
        left = l_ref[s]
        both = jnp.concatenate([left, left], axis=0)
        spec = lax.dot_general(fwd_ref[...], both, nt, preferred_element_type=F32)
        lenergy[...] += jnp.sum((spec * spec).reshape(2 * NF // 8, 8, 2 * rows), axis=0)
        base = pl.multiple_of(s * 2 * PITCH, 8)
        top, bottom = spec[:NF], spec[NF:]
        lspec[pl.ds(base, NF), :] = jnp.where(lane < rows, top, -bottom)
        lspec[pl.ds(base + PITCH, NF), :] = jnp.where(lane < rows, bottom, top)

    for k in range(segs):
        hop_a[k].start()
    ask.wait_recv()
    for step in range(segs + 4):
        k = step
        if k < segs:
            mine[k].wait()
            hop_a[k].wait_recv()
            near[k] = pick(wish[0:1, :], far[k], own[k])
            hop_b[k].start()
        k = step - 1
        if 0 <= k < segs:
            hop_b[k].wait_recv()
            r_ref[t * segs + k] = pick(take_r, got[k], own[k])
            to_y[k].start()
            lsend[k] = pick(take_l, got[k], own[k])
            for copy in parts[k]:
                copy.start()
            to_core[k].start()
            l_ref[t * segs + k] = lsend[k, pl.ds(pl.multiple_of(t * rows, rows), rows)]
            spectra_r(t * segs + k)
            spectra_l(t * segs + k)
        k = step - 3
        if 0 <= k < segs:
            to_y[k].wait_recv()
            forward[k].start()
            to_core[k].wait_recv()
            spectra_r(t1 * segs + k)
            parts[k][2].wait_recv()
            spectra_l(t1 * segs + k)
            spectra_r(t2 * segs + k)
        k = step - 4
        if 0 <= k < segs:
            parts[k][0].wait_recv()
            spectra_l(t2 * segs + k)
            parts[k][1].wait_recv()
            spectra_l(t3 * segs + k)
            forward[k].wait_recv()
            spectra_r(t3 * segs + k)
    ask.wait_send()
    for k in range(segs):
        hop_a[k].wait_send()
        hop_b[k].wait_send()
        to_y[k].wait_send()
        to_core[k].wait_send()
        forward[k].wait_send()
        for copy in parts[k]:
            copy.wait_send()

    count = count_ref[0]
    rscale = 1.0 / jnp.sqrt(jnp.sum(renergy[...], axis=0, keepdims=True) / (nseg * NF) + 1e-06)
    lscale = 1.0 / jnp.sqrt(jnp.sum(lenergy[...], axis=0, keepdims=True) / (nseg * NF) + 1e-06)
    seg_of = lax.broadcasted_iota(jnp.int32, (2 * nseg, 2 * rows), 0) // 2
    lscale = jnp.where(seg_of < count, jnp.broadcast_to(lscale, (2 * nseg, 2 * rows)), 0.0)

    def one_bin(f, _):
        right = jnp.concatenate(
            [rspec[pl.ds(h * span + f, 2 * nseg, stride=PITCH), :] for h in range(halves)], axis=1)
        right = (right * rscale).astype(BF16)
        left = (lspec[pl.ds(f, 2 * nseg, stride=PITCH), :] * lscale).astype(BF16)
        both = lax.dot_general(
            left, right, (((0,), (0,)), ((), ())), preferred_element_type=F32)
        base = pl.multiple_of(f * PITCH, 8)
        for h in range(halves):
            cross[pl.ds(h * depth + base, 2 * rows), :] = both[:, h * LANES:(h + 1) * LANES]
        return 0

    lax.fori_loop(0, NF, one_bin, 0, unroll=8)
    share = 1.0 / jnp.maximum(count, 1).astype(F32)

    def one_row(i, _):
        for h in range(halves):
            real = cross[pl.ds(h * depth + i, NF, stride=PITCH), :].astype(BF16)
            imag = cross[pl.ds(h * depth + rows + i, NF, stride=PITCH), :].astype(BF16)
            both = jnp.concatenate([real, imag], axis=0)
            corr = jnp.dot(inv_ref[...], both, preferred_element_type=F32) * share
            out[i, pl.ds(h * LANES, LANES), :] = corr.T.astype(BF16)
        return 0

    parts_out = 4
    piece = rows // parts_out
    copies = []
    for g in range(parts_out):
        lax.fori_loop(g * piece, (g + 1) * piece, one_row, 0, unroll=8)
        copy = pltpu.make_async_copy(out.at[pl.ds(g * piece, piece)],
                                     o_ref.at[pl.ds(g * piece, piece)], o_sem.at[g])
        copy.start()
        copies.append(copy)
    for copy in copies:
        copy.wait()


def body(nchan, traces, tile_list, seg_counts):
    segs, block, samples = traces.shape
    ntm = 4
    nseg = segs * ntm
    rows = block // ntm
    vmem = pl.BlockSpec(memory_space=pltpu.VMEM)
    smem = pl.BlockSpec(memory_space=pltpu.SMEM)
    hbm = pl.BlockSpec(memory_space=pl.ANY)
    dma = pltpu.SemaphoreType.DMA
    halves = block // LANES
    out = pl.pallas_call(
        functools.partial(kernel, nchan),
        out_shape=jax.ShapeDtypeStruct((rows, block, LAGS), BF16),
        in_specs=[smem, smem, hbm, vmem, vmem],
        out_specs=hbm,
        scratch_shapes=[pltpu.VMEM((segs, block, samples), BF16)] * 5 + [
            pltpu.VMEM((8, samples), jnp.int32), pltpu.VMEM((8, samples), jnp.int32),
            pltpu.VMEM((nseg, block, samples), BF16),
            pltpu.VMEM((nseg, rows, samples), BF16),
            pltpu.VMEM((halves * nseg * 2 * PITCH, LANES), F32),
            pltpu.VMEM((nseg * 2 * PITCH, 2 * rows), F32),
            pltpu.VMEM((8, block), F32), pltpu.VMEM((8, 2 * rows), F32),
            pltpu.VMEM((halves * NF * PITCH, LANES), F32),
            pltpu.VMEM((rows, block, LAGS), BF16),
            dma((segs,)), dma((segs,)), dma((segs,)), dma((segs,)), dma((segs,)), dma, dma,
            dma((3, segs)), dma((3, segs)), dma((3, segs)), dma((3, segs)), dma((4,))],
        compiler_params=pltpu.CompilerParams(
            collective_id=0, has_side_effects=True, vmem_limit_bytes=58 << 20),
        name="correlate",
    )(tile_list, seg_counts, traces, forward_table(samples, NF), inverse_table(samples, NF, LAGS))
    return out[None]


def solution(mesh):
    return jax.shard_map(
        functools.partial(body, mesh.shape["chan"]),
        mesh=mesh,
        in_specs=(P("tm", "chan", None), P("chan", None), P("chan")),
        out_specs=P("chan", "tm", None, None),
        check_vma=False,
    )
```

```python
import functools
import math

import jax
import jax.numpy as jnp
import numpy as np
from jax import lax
from jax.experimental import pallas as pl
from jax.experimental.pallas import tpu as pltpu
from jax.sharding import PartitionSpec as P

NF = 128
LAGS = 128
LANES = 128
PITCH = NF + 8
OUT_PITCH = NF + 4
LIMIT = 40
MESH = pl.DeviceIdType.MESH
F32 = jnp.float32
BF16 = jnp.bfloat16


def forward_table(samples, nbins):
    n_idx = np.arange(samples)[None, :]
    k_idx = np.arange(1, nbins + 1)[:, None]
    phase = (n_idx * k_idx % samples).astype(np.float32) * np.float32(2.0 * math.pi / samples)
    return jnp.asarray(np.concatenate([np.cos(phase), -np.sin(phase)], axis=0), BF16)


def inverse_table(samples, nbins, nlags):
    k_idx = np.arange(1, nbins + 1)[None, :]
    lag_idx = np.arange(nlags)[:, None] - nlags // 2
    phase = (k_idx * lag_idx % samples).astype(np.float32) * np.float32(2.0 * math.pi / samples)
    norm = np.float32(1.0 / math.sqrt(nbins))
    return jnp.asarray(np.concatenate([np.cos(phase), -np.sin(phase)], axis=1) * norm, BF16)


def pick(flag, yes, no):
    return jnp.where(flag > 0, yes.astype(F32), no.astype(F32)).astype(BF16)


def kernel(nchan, tile_ref, count_ref, x_ref, fwd_ref, inv_ref, o_ref,
           own, far, near, got, lsend, asked, wish, r_ref, l_ref, rspec, lspec, renergy, lenergy,
           cross, own_sem, a_send, a_recv, b_send, b_recv, w_send, w_recv,
           r_send, r_recv, l_send, l_recv):
    segs, block, samples = own.shape
    nseg = r_ref.shape[0]
    rows = block // 4
    halves = block // LANES
    span = nseg * 2 * PITCH
    c = lax.axis_index("chan")
    t = lax.axis_index("tm")
    odd = lax.rem(c, 2)
    partner = c + 1 - 2 * odd
    z_to = lax.rem(c + nchan - 2 + 4 * odd, nchan)
    z_from = lax.rem(c + nchan + 2 - 4 * odd, nchan)
    core = lax.rem(t, 2)
    t1 = t + 1 - 2 * core
    t2 = lax.rem(t + 2, 4)
    t3 = lax.rem(t1 + 2, 4)

    mine = [pltpu.make_async_copy(x_ref.at[k], own.at[k], own_sem.at[k]) for k in range(segs)]
    for copy in mine:
        copy.start()
    row_b, col_b = tile_ref[0, 0], tile_ref[0, 1]
    beyond = jnp.where(odd == 1, jnp.maximum(row_b, col_b) - c, c - jnp.minimum(row_b, col_b))
    asked[...] = jnp.full(asked.shape, beyond, jnp.int32)
    take_r = jnp.full((1, samples), (col_b - c) * (col_b - c), jnp.int32)
    take_l = jnp.full((1, samples), (row_b - c) * (row_b - c), jnp.int32)
    renergy[...] = jnp.zeros_like(renergy)
    lenergy[...] = jnp.zeros_like(lenergy)

    barrier = pltpu.get_barrier_semaphore()
    for where in ((z_to, t), (z_from, t), (partner, t), (c, t1), (c, t2), (c, t3)):
        pl.semaphore_signal(barrier, inc=1, device_id=where, device_id_type=MESH)
    pl.semaphore_wait(barrier, 6)

    def send(src, dst, ss, rs, where):
        return pltpu.make_async_remote_copy(
            src_ref=src, dst_ref=dst, send_sem=ss, recv_sem=rs,
            device_id=where, device_id_type=MESH)

    ask = send(asked, wish, w_send, w_recv, (partner, t))
    ask.start()
    hop_a = [send(x_ref.at[k], far.at[k], a_send.at[k], a_recv.at[k], (z_to, t))
             for k in range(segs)]
    hop_b = [send(near.at[k], got.at[k], b_send.at[k], b_recv.at[k], (partner, t))
             for k in range(segs)]

    def share(k, h, slot, which, where):
        ref = r_ref.at[slot * segs + k, pl.ds(h * LANES, LANES)]
        return send(ref, ref, r_send.at[which, h, k], r_recv.at[which, h, k], where)

    def share_l(k, which, peer):
        return send(lsend.at[k, pl.ds(pl.multiple_of(peer * rows, rows), rows)],
                    l_ref.at[t * segs + k],
                    l_send.at[which, k], l_recv.at[which, k], (c, peer))

    to_y = [[share(k, h, t, 0, (c, t2)) for k in range(segs)] for h in range(halves)]
    to_core = [[share(k, h, t, 1, (c, t1)) for k in range(segs)] for h in range(halves)]
    forward = [[share(k, h, t2, 2, (c, t1)) for k in range(segs)] for h in range(halves)]
    parts = [[share_l(k, w, p) for w, p in enumerate((t2, t3, t1))] for k in range(segs)]

    nt = (((1,), (1,)), ((), ()))
    lane = lax.broadcasted_iota(jnp.int32, (1, 2 * rows), 1)

    def spectra_r(s, h):
        spec = lax.dot_general(fwd_ref[...], r_ref[s, pl.ds(h * LANES, LANES)], nt,
                               preferred_element_type=F32)
        base = pl.multiple_of(h * span + s * 2 * PITCH, 8)
        rspec[pl.ds(base, NF), :] = spec[:NF]
        rspec[pl.ds(base + PITCH, NF), :] = spec[NF:]
        renergy[h] += jnp.sum((spec * spec).reshape(2 * NF // 8, 8, LANES), axis=0)

    def spectra_l(s):
        left = l_ref[s]
        both = jnp.concatenate([left, left], axis=0)
        spec = lax.dot_general(fwd_ref[...], both, nt, preferred_element_type=F32)
        lenergy[...] += jnp.sum((spec * spec).reshape(2 * NF // 8, 8, 2 * rows), axis=0)
        base = pl.multiple_of(s * 2 * PITCH, 8)
        top, bottom = spec[:NF], spec[NF:]
        lspec[pl.ds(base, NF), :] = jnp.where(lane < rows, top, -bottom)
        lspec[pl.ds(base + PITCH, NF), :] = jnp.where(lane < rows, bottom, top)

    for k in range(segs):
        hop_a[k].start()
    ask.wait_recv()
    for step in range(segs + 4):
        k = step
        if k < segs:
            mine[k].wait()
            hop_a[k].wait_recv()
            near[k] = pick(wish[0:1, :], far[k], own[k])
            hop_b[k].start()
        k = step - 1
        if 0 <= k < segs:
            hop_b[k].wait_recv()
            r_ref[t * segs + k] = pick(take_r, got[k], own[k])
            to_y[0][k].start()
            lsend[k] = pick(take_l, got[k], own[k])
            for copy in parts[k]:
                copy.start()
            to_core[0][k].start()
            l_ref[t * segs + k] = lsend[k, pl.ds(pl.multiple_of(t * rows, rows), rows)]
            if k == segs - 1:
                for h in range(1, halves):
                    for i in range(segs):
                        to_y[h][i].start()
                        to_core[h][i].start()
            spectra_r(t * segs + k, 0)
            spectra_l(t * segs + k)
        k = step - 3
        if 0 <= k < segs:
            to_y[0][k].wait_recv()
            forward[0][k].start()
            to_core[0][k].wait_recv()
            spectra_r(t1 * segs + k, 0)
            parts[k][2].wait_recv()
            spectra_l(t1 * segs + k)
            spectra_r(t2 * segs + k, 0)
        k = step - 4
        if 0 <= k < segs:
            parts[k][0].wait_recv()
            spectra_l(t2 * segs + k)
            parts[k][1].wait_recv()
            spectra_l(t3 * segs + k)
            forward[0][k].wait_recv()
            spectra_r(t3 * segs + k, 0)

    count = count_ref[0]
    lscale = 1.0 / jnp.sqrt(jnp.sum(lenergy[...], axis=0, keepdims=True) / (nseg * NF) + 1e-06)
    seg_of = lax.broadcasted_iota(jnp.int32, (2 * nseg, 2 * rows), 0) // 2
    lscale = jnp.where(seg_of < count, jnp.broadcast_to(lscale, (2 * nseg, 2 * rows)), 0.0)
    share_n = 1.0 / jnp.maximum(count, 1).astype(F32)

    def stack(h):
        rscale = jnp.sum(renergy[h], axis=0, keepdims=True) / (nseg * NF) + 1e-06
        rscale = 1.0 / jnp.sqrt(rscale)

        def one_bin(f, _):
            right = rspec[pl.ds(h * span + f, 2 * nseg, stride=PITCH), :]
            right = (right * rscale).astype(BF16)
            left = (lspec[pl.ds(f, 2 * nseg, stride=PITCH), :] * lscale).astype(BF16)
            cross[pl.ds(f * OUT_PITCH, 2 * rows), :] = lax.dot_general(
                left, right, (((0,), (0,)), ((), ())), preferred_element_type=F32)
            return 0

        lax.fori_loop(0, NF, one_bin, 0, unroll=16)

    def lags(h, first, last):
        def one_row(i, _):
            real = cross[pl.ds(i, NF, stride=OUT_PITCH), :].astype(BF16)
            imag = cross[pl.ds(rows + i, NF, stride=OUT_PITCH), :].astype(BF16)
            both = jnp.concatenate([real, imag], axis=0)
            corr = jnp.dot(inv_ref[...], both, preferred_element_type=F32) * share_n
            o_ref[i, pl.ds(h * LANES, LANES), :] = corr.T.astype(BF16)
            return 0

        lax.fori_loop(first, last, one_row, 0, unroll=16)

    stack(0)
    for h in range(1, halves):
        for k in range(segs // 2):
            to_y[h][k].wait_recv()
            forward[h][k].start()
        lags(h - 1, 0, rows)
        for k in range(segs // 2, segs):
            to_y[h][k].wait_recv()
            forward[h][k].start()
            spectra_r(t * segs + k, h)
            spectra_r(t * segs + k - segs // 2, h)
            to_core[h][k].wait_recv()
            to_core[h][k - segs // 2].wait_recv()
            spectra_r(t1 * segs + k, h)
            spectra_r(t1 * segs + k - segs // 2, h)
            spectra_r(t2 * segs + k - segs // 2, h)
            forward[h][k - segs // 2].wait_recv()
            spectra_r(t3 * segs + k - segs // 2, h)
        for k in range(segs // 2, segs):
            spectra_r(t2 * segs + k, h)
            forward[h][k].wait_recv()
            spectra_r(t3 * segs + k, h)
        stack(h)
    lags(halves - 1, 0, rows)

    ask.wait_send()
    for k in range(segs):
        hop_a[k].wait_send()
        hop_b[k].wait_send()
        for h in range(halves):
            to_y[h][k].wait_send()
            to_core[h][k].wait_send()
            forward[h][k].wait_send()
        for copy in parts[k]:
            copy.wait_send()


def body(nchan, traces, tile_list, seg_counts):
    segs, block, samples = traces.shape
    ntm = 4
    nseg = segs * ntm
    rows = block // ntm
    vmem = pl.BlockSpec(memory_space=pltpu.VMEM)
    smem = pl.BlockSpec(memory_space=pltpu.SMEM)
    hbm = pl.BlockSpec(memory_space=pltpu.HBM)
    dma = pltpu.SemaphoreType.DMA
    halves = block // LANES
    out = pl.pallas_call(
        functools.partial(kernel, nchan),
        out_shape=jax.ShapeDtypeStruct((rows, block, LAGS), BF16),
        in_specs=[smem, smem, hbm, vmem, vmem],
        out_specs=vmem,
        scratch_shapes=[pltpu.VMEM((segs, block, samples), BF16)] * 5 + [
            pltpu.VMEM((8, samples), jnp.int32), pltpu.VMEM((8, samples), jnp.int32),
            pltpu.VMEM((nseg, block, samples), BF16),
            pltpu.VMEM((nseg, rows, samples), BF16),
            pltpu.VMEM((halves * nseg * 2 * PITCH, LANES), F32),
            pltpu.VMEM((nseg * 2 * PITCH, 2 * rows), F32),
            pltpu.VMEM((halves, 8, LANES), F32), pltpu.VMEM((8, 2 * rows), F32),
            pltpu.VMEM((NF * OUT_PITCH, LANES), F32),
            dma((segs,)), dma((segs,)), dma((segs,)), dma((segs,)), dma((segs,)), dma, dma,
            dma((3, halves, segs)), dma((3, halves, segs)), dma((3, segs)), dma((3, segs))],
        compiler_params=pltpu.CompilerParams(
            collective_id=0, has_side_effects=True, vmem_limit_bytes=LIMIT << 20),
        name="correlate",
    )(tile_list, seg_counts, traces, forward_table(samples, NF), inverse_table(samples, NF, LAGS))
    return out[None]


def solution(mesh):
    return jax.shard_map(
        functools.partial(body, mesh.shape["chan"]),
        mesh=mesh,
        in_specs=(P("tm", "chan", None), P("chan", None), P("chan")),
        out_specs=P("chan", "tm", None, None),
        check_vma=False,
    )
```
